32 devices in a mesh: groups: 2 (over y), brick: 16 (over z, x, core), frame: 1.
Axes of the slice: x: 2, y: 2, z: 4, core: 2. Of those that a mesh axis runs over, the one named last changes fastest.
Arguments:
- volume: float32 [4, 128, 32, 512], P(('groups', 'frame'), 'brick'), parts along dimension 0, may hold values from -6 to 6
- offsets: int32 [128, 3], P(('groups', 'brick')), parts along dimension 0, may hold values from -8 to 8
Outputs:
- correlation: float32 [128, 32, 32, 32], P(('groups', 'brick', 'frame')), parts along dimension 0
The draws below stay inside these ranges and needn't reach their ends.
There are 2 independent parts, one for each index of `groups`. The reference program is written for one: setup_inputs(seed, part) draws one part's arguments, and reference() takes and returns one part's arrays. A program takes and returns all parts, laid end to end along the dimension named above; each array names one. Nothing has to cross between parts.
All inputs are finite; a program needn't handle non-finite values.
Results may differ from the reference program's by a relative error of at most 0.0003.
Values sent between devices are 32-bit elements; how exact they have to be, the bound alone decides.
A program may use at most 192 MiB of HBM per device.

```python
import jax
import jax.numpy as jnp
from jax import lax

W = 32
H = 8
BX = 16
ZB = 4
FRAMES = 2
Z = 128
NX = 512
NY = 32
BRICKS = 64


def with_ends(array, own_key, smallest, high):
    longest = array.shape.index(max(array.shape))
    spots = []
    for shift in (0, 1):
        where = [jax.random.randint(jax.random.fold_in(own_key, axis), (), 0, length) for axis, length in enumerate(array.shape)]
        where[longest] = (where[longest] + shift) % array.shape[longest]
        spots.append(tuple(where))
    return array.at[spots[0]].set(smallest).at[spots[1]].set(high)


def level_of(rng, shape, cuts, low, top_value):
    factor_of, own = 1.0, jax.random.fold_in(rng, 6)
    for dim, parts in cuts:
        heights = jnp.exp(jax.random.uniform(jax.random.fold_in(own, dim), (parts,), jnp.float32, low / len(cuts), top_value / len(cuts)))
        factor_of = factor_of * jnp.repeat(heights, shape[dim] // parts).reshape([-1 if axis == dim else 1 for axis in range(len(shape))])
    return factor_of


def centred(rng, extent, spread, limit, cuts=(), kind=jnp.bfloat16):
    level = level_of(rng, extent, cuts, -0.22, 0.18) if cuts else 1.0
    drawn = jax.random.normal(rng, extent, jnp.float32) * spread * level
    return jnp.minimum(jnp.maximum(drawn, -limit), limit).astype(kind)


def setup_inputs(seed: int = 0, part: int = 0) -> dict:
    seeds = jax.random.split(jax.random.key(seed), 3)
    part_keys = jax.random.split(jax.random.fold_in(seeds[2], part), 3)
    return {
        "volume": centred(part_keys[0], (FRAMES, Z, NY, NX), 1.0, 6.0, ((1, 16),), jnp.float32),
        "offsets": with_ends(jax.random.randint(part_keys[1], (BRICKS, 3), -H, H + 1), jax.random.fold_in(part_keys[1], 1), -H, H).astype(jnp.int32),
    }


def taper_table(width):
    position = jnp.arange(width).astype(jnp.float32)
    return 0.5 - 0.5 * jnp.cos(2.0 * jnp.pi * (position + 0.5) / width)


def reference(volume, offsets):
    frames = volume.shape[0]
    padded = jnp.pad(volume, ((0, 0), (H, H), (H, H), (H, H)))
    taper = taper_table(W)
    weight3 = taper[:, None, None] * taper[None, :, None] * taper[None, None, :]
    scale = 4.0 / (W ** 1.5)

    def one_brick(index):
        column = index // ZB
        depth = index % ZB
        start_z = (depth * W).astype(jnp.int32)
        start_y = ((column // BX) * W).astype(jnp.int32)
        start_x = ((column % BX) * W).astype(jnp.int32)
        zero = jnp.zeros((), jnp.int32)
        first = lax.dynamic_slice(volume, (zero, start_z, start_y, start_x), (frames, W, W, W))
        shift = offsets[index].astype(jnp.int32)
        second = lax.dynamic_slice(padded, (zero, start_z + H + shift[0], start_y + H + shift[1], start_x + H + shift[2]), (frames, W, W, W))
        spec_a = jnp.fft.fftn(first * weight3, axes=(1, 2, 3))
        spec_b = jnp.fft.fftn(second * weight3, axes=(1, 2, 3))
        total = jnp.sum(jnp.conj(spec_a[:-1]) * spec_b[1:], axis=0)
        total = total + jnp.sum(jnp.conj(spec_a[:-2]) * spec_b[2:], axis=0)
        return jnp.real(jnp.fft.ifftn(total)) * scale

    return lax.map(one_brick, jnp.arange(BRICKS).astype(jnp.int32))
```

```python
import functools

import jax
import jax.numpy as jnp
import ml_dtypes
import numpy as np
from jax import lax
from jax.experimental import pallas as pl
from jax.experimental.pallas import tpu as pltpu
from jax.sharding import PartitionSpec as P

W = 32
H = 8
COLS_DEV = 1
ZB = 4


HIGHEST = lax.Precision.HIGHEST


def from_behind(shard, axis, by):
    count = lax.axis_size(axis)
    pairs = [(i, i + by) for i in range(count) if 0 <= i + by < count]
    return lax.ppermute(shard, axis, pairs)


def taper_table(width):
    position = jnp.arange(width).astype(jnp.float32)
    return 0.5 - 0.5 * jnp.cos(2.0 * jnp.pi * (position + 0.5) / width)


def fourier_tables(width):
    index = jnp.arange(width)
    product = index[:, None] * index[None, :] % width
    angle = 2.0 * jnp.pi * product.astype(jnp.float32) / width
    return (jnp.cos(angle), jnp.sin(angle))


def plane_tables(width):
    index = jnp.arange(width * width)
    upper = index // width
    lower = index % width
    product = (upper[:, None] * upper[None, :] + lower[:, None] * lower[None, :]) % width
    angle = 2.0 * jnp.pi * product.astype(jnp.float32) / width
    return (jnp.cos(angle), jnp.sin(angle))


def depth_apply(table, values):
    return jnp.einsum("kz,nzm->nkm", table, values, precision=HIGHEST)


def plane_apply(values, table):
    count, depth, plane = values.shape
    flat = values.reshape(count * depth, plane)
    result = jnp.dot(flat, table, precision=HIGHEST, preferred_element_type=jnp.float32)
    return result.reshape(count, depth, plane)


def forward(field, tables):
    cosine, sine, plane_cos, plane_sin = tables
    count, width = (field.shape[0], field.shape[1])
    values = field.reshape(count, width, width * width)
    real_part = plane_apply(values, plane_cos)
    imag_part = -plane_apply(values, plane_sin)
    return (
        depth_apply(cosine, real_part) + depth_apply(sine, imag_part),
        depth_apply(cosine, imag_part) - depth_apply(sine, real_part),
    )


def inverse_real(real_part, imag_part, tables):
    cosine, sine, plane_cos, plane_sin = tables
    first_re = depth_apply(cosine, real_part) - depth_apply(sine, imag_part)
    first_im = depth_apply(cosine, imag_part) + depth_apply(sine, real_part)
    result = plane_apply(first_re, plane_cos) - plane_apply(first_im, plane_sin)
    width = result.shape[1]
    return result.reshape(result.shape[0], width, width, width)


def column_pieces(slabs):
    count, planes, rows, cols = slabs.shape
    span = COLS_DEV * W
    tiles = slabs.reshape(count, planes, rows // W, W, cols // span, span)
    tiles = jnp.pad(tiles, ((0, 0), (0, 0), (1, 1), (0, 0), (1, 1), (0, 0)))
    tall = jnp.concatenate([tiles[:, :, :-2, W - H :], tiles[:, :, 1:-1], tiles[:, :, 2:, :H]], 3)
    wide = jnp.concatenate(
        [tall[:, :, :, :, :-2, span - H :], tall[:, :, :, :, 1:-1], tall[:, :, :, :, 2:, :H]], 5
    )
    wide = jnp.transpose(wide, (0, 1, 2, 4, 3, 5))
    owners = rows // W * (cols // span)
    return wide.reshape(count, planes, owners, (W + 2 * H) * (span + 2 * H))


def merge_depth(received):
    count = received.shape[0]
    depth_total = received.shape[1] * received.shape[2]
    merged = received.reshape(count, depth_total, W + 2 * H, COLS_DEV * W + 2 * H)
    return jnp.pad(merged, ((0, 0), (H, H), (0, 0), (0, 0)))


def cross_sum(first, paired):
    first_re, first_im = first
    paired_re, paired_im = paired
    spectrum_re = jnp.sum(first_re * paired_re + first_im * paired_im, axis=0)
    spectrum_im = jnp.sum(first_re * paired_im - first_im * paired_re, axis=0)
    return (spectrum_re, spectrum_im)


def shards(volume, offsets):
    frames_here = volume.shape[0]
    taper = taper_table(W)
    weight3 = taper[:, None, None] * taper[None, :, None] * taper[None, None, :]
    cosine, sine = fourier_tables(W)
    plane_cos, plane_sin = plane_tables(W)
    tables = (cosine, sine, plane_cos, plane_sin)
    factor = 4.0 / W**1.5 / W**3

    def transformed(fields, moves, depth_rel, col_rel):

        def windows(frame_field):

            def one_window(depth, column, move):
                return lax.dynamic_slice(
                    frame_field,
                    (H + depth * W + move[0], H + move[1], H + column * W + move[2]),
                    (W, W, W),
                )

            return jax.vmap(one_window)(depth_rel, col_rel, moves) * weight3

        cut = jax.vmap(windows)(fields)
        frame_total, count = (cut.shape[0], cut.shape[1])
        real_part, imag_part = forward(cut.reshape(frame_total * count, W, W, W), tables)
        return (
            real_part.reshape(frame_total, count, W, W * W),
            imag_part.reshape(frame_total, count, W, W * W),
        )

    columns = lax.all_to_all(
        column_pieces(volume), "brick", split_axis=2, concat_axis=1, tiled=True
    )
    following = from_behind(columns, "frame", -1)
    stacked = jnp.concatenate([columns, following], 0)
    stacked = merge_depth(stacked)
    local_count = offsets.shape[0]
    local_index = jnp.arange(local_count)
    depth_index = local_index % ZB
    column_local = local_index // ZB
    first = transformed(stacked[:frames_here], jnp.zeros_like(offsets), depth_index, column_local)
    second_re, second_im = transformed(stacked[1:], offsets, depth_index, column_local)
    paired_re = second_re[:-1] + second_re[1:]
    paired_im = second_im[:-1] + second_im[1:]
    spectrum_re, spectrum_im = cross_sum(first, (paired_re, paired_im))
    share_re, share_im = (
        lax.psum_scatter(spectrum_re, "frame", scatter_dimension=0, tiled=True),
        lax.psum_scatter(spectrum_im, "frame", scatter_dimension=0, tiled=True),
    )
    return inverse_real(share_re, share_im, tables) * factor


KB = 3
T = 8


def halves(table):
    table = np.asarray(table, np.float32)
    high = table.astype(ml_dtypes.bfloat16)
    low = (table - high.astype(np.float32)).astype(ml_dtypes.bfloat16)
    return np.stack([high, low])


def fixed_tables():
    index = np.arange(W)
    angle = 2.0 * np.pi * (index[:, None] * index[None, :] % W) / W
    cosine, sine = np.cos(angle), np.sin(angle)
    unit = np.eye(T)
    kept = np.zeros((KB * T, W))
    kept[: W // 2 + 1, : W // 2 + 1] = np.eye(W // 2 + 1)
    parts = np.stack([kept @ cosine, -(kept @ sine)]).reshape(2, KB, T, W)
    along_y = np.einsum("rbky,zs->rbzksy", parts, unit).reshape(2 * KB * T * T, T * W)
    weight = np.where((index == 0) | (index == W // 2), 1.0, 2.0)[:, None]
    factor = 4.0 / W**1.5 / W**3
    parts = factor * np.stack([kept @ (weight * cosine), -(kept @ (weight * sine))]).reshape(2, KB, T, W)
    back_y = np.einsum("rbky,zs->zyrbsk", parts, unit).reshape(T * W, 2 * KB * T * T)
    along_z = np.kron(np.block([[cosine, sine], [-sine, cosine]]), unit)
    four = np.eye(ZB)
    along_x = np.block([[np.kron(four, cosine), -np.kron(four, sine)], [np.kron(four, sine), np.kron(four, cosine)]])
    taper = 0.5 - 0.5 * np.cos(2.0 * np.pi * (index + 0.5) / W)
    lanes = np.tile(taper, ZB)
    weight3 = (taper[:, None, None] * taper[None, :, None] * lanes[None, None, :]).astype(np.float32)
    lane = np.arange(128)
    brick = np.arange(ZB)[:, None]
    main = (brick * 4 + lane // W) * 64 + lane % W + H
    edge = lane % 16
    halo = (brick * 4 + lane % 64 // 16) * 64 + np.where(edge < H, edge, edge + W)
    row_key = np.concatenate([main.reshape(-1), halo.reshape(-1)]).astype(np.int32)[:, None]
    return (
        halves(along_y), halves(along_z), halves(along_x),
        halves(along_x.T), halves(along_z.T), halves(back_y),
        weight3, row_key,
    )


def split(values):
    high = values.astype(jnp.bfloat16)
    return high, (values - high.astype(jnp.float32)).astype(jnp.bfloat16)


def mul(left, right):
    return jnp.dot(left, right, preferred_element_type=jnp.float32)


def from_left(table, values):
    high, low = split(values)
    return mul(table[0], high) + mul(table[0], low) + mul(table[1], high)


def from_right(values, table):
    high, low = split(values)
    return mul(high, table[0]) + mul(low, table[0]) + mul(high, table[1])


def pack(volume, send):
    columns = send.shape[0]
    for c in range(columns):
        at = c * W
        for f in range(2):
            parts = [volume[f, :, T * j : T * j + T, at : at + W] for j in range(4)]
            send[c, T * f : T * f + T] = jnp.concatenate(parts, -1)
        parts = []
        for zh in range(2):
            for j in range(4):
                for start in (at - H, at + W):
                    if 0 <= start < columns * W:
                        parts.append(volume[1, 4 * zh : 4 * zh + 4, T * j : T * j + T, start : start + H])
                    else:
                        parts.append(jnp.zeros((4, T, H), jnp.float32))
        send[c, 2 * T :] = jnp.concatenate(parts, -1)


def first_windows(held, row_key, field):
    lane = lax.broadcasted_iota(jnp.int32, (1, 4 * 128), 1)
    col_key = (lane // W % 4 * 4 + lane // 128) * 64 + lane % W + H
    chosen = (row_key[0:512] == col_key).astype(jnp.float32).astype(jnp.bfloat16)
    rows = jnp.concatenate([held[4 * q : 4 * q + 4, 0:T].reshape(W * T, 128) for q in range(ZB)], -1)
    high, low = split(rows)
    moved = mul(high, chosen) + mul(low, chosen)
    for j in range(4):
        field[:, T * j : T * j + T, 0:128] = moved[:, 128 * j : 128 * j + 128].reshape(W, T, 128)


def second_windows(held, offsets, row_key, main, halo, spread, field):
    lane = lax.broadcasted_iota(jnp.int32, (1, 4 * 128), 1)
    brick = lane // W % 4
    shift = jnp.zeros((1, 4 * 128), jnp.int32)
    for q in range(ZB):
        shift = jnp.where(brick == q, offsets[q, 2], shift)
    col_key = (brick * 4 + lane // 128) * 64 + lane % W + H + shift
    chosen = (row_key[...] == col_key).astype(jnp.float32).astype(jnp.bfloat16)
    depth = main.shape[0] - 2 * H
    for ref in (main, halo):
        ref[0:H] = jnp.zeros((H, T, 128), jnp.float32)
        ref[H + depth :] = jnp.zeros((H, T, 128), jnp.float32)
    upper = lax.broadcasted_iota(jnp.int32, (1, 1, 1, 128), 3) >= 64
    slabs = held.shape[0]
    main[H : H + depth] = held[:, T : 2 * T].reshape(depth, T, 128)
    edges = held[:, 2 * T :]
    both = jnp.concatenate([jnp.where(upper, 0.0, edges), jnp.where(upper, edges, 0.0)], 1)
    halo[H : H + depth] = both.reshape(depth, T, 128)
    span = W + 2 * H
    rows = [ref[W * q : W * q + span].reshape(span * T, 128) for ref in (main, halo) for q in range(ZB)]
    high, low = split(jnp.concatenate(rows, -1))
    moved = mul(high, chosen) + mul(low, chosen)
    spread[:, 0:H] = jnp.zeros((span, H, 128), jnp.float32)
    spread[:, H + W :] = jnp.zeros((span, H, 128), jnp.float32)
    for j in range(4):
        spread[:, H + T * j : H + T * j + T] = moved[:, 128 * j : 128 * j + 128].reshape(span, T, 128)
    own = lax.broadcasted_iota(jnp.int32, (1, 1, 128), 2) // W
    cut = jnp.zeros((W, W, 128), jnp.float32)
    for q in range(ZB):
        window = spread[pl.ds(H + offsets[q, 0], W), pl.ds(H + offsets[q, 1], W), :]
        cut = jnp.where(own == q, window, cut)
    field[:, :, 128:256] = cut


def correlate(field, weight3, tables, mid, back, out):
    along_y, along_z, along_x, back_x, back_z, back_y = tables
    block = T * T
    for zb in range(4):
        weight = weight3[T * zb : T * zb + T]
        tapered = field[T * zb : T * zb + T] * jnp.concatenate([weight, weight], -1)
        part = from_left(along_y, tapered.reshape(T * W, 256))
        for r in range(2):
            for b in range(KB):
                at = (r * KB + b) * block
                mid[b, (r * 4 + zb) * block : (r * 4 + zb + 1) * block] = part[at : at + block]
    half = W * T
    for b in range(KB):
        spec = from_left(along_z, mid[b])
        first, second = (
            from_right(jnp.concatenate([spec[:half, s], spec[half:, s]], -1), along_x)
            for s in (slice(0, 128), slice(128, 256))
        )
        first_re, first_im = first[:, :128], first[:, 128:]
        second_re, second_im = second[:, :128], second[:, 128:]
        real_part = first_re * second_re + first_im * second_im
        imag_part = first_re * second_im - first_im * second_re
        lines = from_right(jnp.concatenate([real_part, imag_part], -1), back_x)
        part = from_left(back_z, jnp.concatenate([lines[:, :128], lines[:, 128:]], 0))
        for r in range(2):
            for zb in range(4):
                at = (r * 4 + zb) * block
                back[zb, (r * KB + b) * block : (r * KB + b + 1) * block] = part[at : at + block]
    for zb in range(4):
        result = from_left(back_y, back[zb]).reshape(T, W, 128)
        for q in range(ZB):
            out[q, T * zb : T * zb + T] = result[:, :, W * q : W * q + W]


def bricks(offsets, held, along_y, along_z, along_x, back_x, back_z, back_y, weight3, row_key, out,
           main, halo, spread, field, mid, back):
    first_windows(held, row_key, field)
    second_windows(held, offsets, row_key, main, halo, spread, field)
    correlate(field, weight3, (along_y, along_z, along_x, back_x, back_z, back_y), mid, back, out)


def two_frames(volume, offsets):
    slabs = lax.axis_size("brick")
    planes = volume.shape[1]
    depth = slabs * planes
    rows = 2 * planes + planes // 2
    vmem = pl.BlockSpec(memory_space=pltpu.VMEM)
    send = pl.pallas_call(
        pack,
        out_shape=jax.ShapeDtypeStruct((slabs, rows, T, 128), jnp.float32),
        in_specs=[vmem],
        out_specs=vmem,
        compiler_params=pltpu.CompilerParams(vmem_limit_bytes=32 << 20),
    )(volume)
    held = lax.all_to_all(send, "brick", split_axis=0, concat_axis=0, tiled=True)
    tables = fixed_tables()
    return pl.pallas_call(
        bricks,
        out_shape=jax.ShapeDtypeStruct((ZB, W, W, W), jnp.float32),
        in_specs=[pl.BlockSpec(memory_space=pltpu.SMEM)] + [vmem] * (1 + len(tables)),
        out_specs=vmem,
        scratch_shapes=[
            pltpu.VMEM((depth + 2 * H, T, 128), jnp.float32),
            pltpu.VMEM((depth + 2 * H, T, 128), jnp.float32),
            pltpu.VMEM((W + 2 * H, W + 2 * H, 128), jnp.float32),
            pltpu.VMEM((W, W, 256), jnp.float32),
            pltpu.VMEM((KB, 2 * W * T, 256), jnp.float32),
            pltpu.VMEM((4, 2 * KB * T * T, 128), jnp.float32),
        ],
        compiler_params=pltpu.CompilerParams(vmem_limit_bytes=48 << 20),
    )(offsets, held, *[jnp.asarray(t) for t in tables])


def per_device(volume, offsets):
    slabs = lax.axis_size("brick")
    frames, planes, rows, cols = volume.shape
    short = lax.axis_size("frame") == 1 and frames == 2 and planes == T and rows == W
    if short and cols == slabs * W and slabs * planes == ZB * W and offsets.shape[0] == ZB:
        return two_frames(volume, offsets)
    return shards(volume, offsets)


def solution(mesh):
    return jax.shard_map(
        per_device,
        mesh=mesh,
        in_specs=(P(("groups", "frame"), "brick", None, None), P(("groups", "brick"), None)),
        out_specs=P(("groups", "brick", "frame"), None, None, None),
        check_vma=False,
    )
```

```python
import functools

import jax
import jax.numpy as jnp
import ml_dtypes
import numpy as np
from jax import lax
from jax.experimental import pallas as pl
from jax.experimental.pallas import tpu as pltpu
from jax.sharding import PartitionSpec as P

W = 32
H = 8
COLS_DEV = 1
ZB = 4


HIGHEST = lax.Precision.HIGHEST


def from_behind(shard, axis, by):
    count = lax.axis_size(axis)
    pairs = [(i, i + by) for i in range(count) if 0 <= i + by < count]
    return lax.ppermute(shard, axis, pairs)


def taper_table(width):
    position = jnp.arange(width).astype(jnp.float32)
    return 0.5 - 0.5 * jnp.cos(2.0 * jnp.pi * (position + 0.5) / width)


def fourier_tables(width):
    index = jnp.arange(width)
    product = index[:, None] * index[None, :] % width
    angle = 2.0 * jnp.pi * product.astype(jnp.float32) / width
    return (jnp.cos(angle), jnp.sin(angle))


def plane_tables(width):
    index = jnp.arange(width * width)
    upper = index // width
    lower = index % width
    product = (upper[:, None] * upper[None, :] + lower[:, None] * lower[None, :]) % width
    angle = 2.0 * jnp.pi * product.astype(jnp.float32) / width
    return (jnp.cos(angle), jnp.sin(angle))


def depth_apply(table, values):
    return jnp.einsum("kz,nzm->nkm", table, values, precision=HIGHEST)


def plane_apply(values, table):
    count, depth, plane = values.shape
    flat = values.reshape(count * depth, plane)
    result = jnp.dot(flat, table, precision=HIGHEST, preferred_element_type=jnp.float32)
    return result.reshape(count, depth, plane)


def forward(field, tables):
    cosine, sine, plane_cos, plane_sin = tables
    count, width = (field.shape[0], field.shape[1])
    values = field.reshape(count, width, width * width)
    real_part = plane_apply(values, plane_cos)
    imag_part = -plane_apply(values, plane_sin)
    return (
        depth_apply(cosine, real_part) + depth_apply(sine, imag_part),
        depth_apply(cosine, imag_part) - depth_apply(sine, real_part),
    )


def inverse_real(real_part, imag_part, tables):
    cosine, sine, plane_cos, plane_sin = tables
    first_re = depth_apply(cosine, real_part) - depth_apply(sine, imag_part)
    first_im = depth_apply(cosine, imag_part) + depth_apply(sine, real_part)
    result = plane_apply(first_re, plane_cos) - plane_apply(first_im, plane_sin)
    width = result.shape[1]
    return result.reshape(result.shape[0], width, width, width)


def column_pieces(slabs):
    count, planes, rows, cols = slabs.shape
    span = COLS_DEV * W
    tiles = slabs.reshape(count, planes, rows // W, W, cols // span, span)
    tiles = jnp.pad(tiles, ((0, 0), (0, 0), (1, 1), (0, 0), (1, 1), (0, 0)))
    tall = jnp.concatenate([tiles[:, :, :-2, W - H :], tiles[:, :, 1:-1], tiles[:, :, 2:, :H]], 3)
    wide = jnp.concatenate(
        [tall[:, :, :, :, :-2, span - H :], tall[:, :, :, :, 1:-1], tall[:, :, :, :, 2:, :H]], 5
    )
    wide = jnp.transpose(wide, (0, 1, 2, 4, 3, 5))
    owners = rows // W * (cols // span)
    return wide.reshape(count, planes, owners, (W + 2 * H) * (span + 2 * H))


def merge_depth(received):
    count = received.shape[0]
    depth_total = received.shape[1] * received.shape[2]
    merged = received.reshape(count, depth_total, W + 2 * H, COLS_DEV * W + 2 * H)
    return jnp.pad(merged, ((0, 0), (H, H), (0, 0), (0, 0)))


def cross_sum(first, paired):
    first_re, first_im = first
    paired_re, paired_im = paired
    spectrum_re = jnp.sum(first_re * paired_re + first_im * paired_im, axis=0)
    spectrum_im = jnp.sum(first_re * paired_im - first_im * paired_re, axis=0)
    return (spectrum_re, spectrum_im)


def shards(volume, offsets):
    frames_here = volume.shape[0]
    taper = taper_table(W)
    weight3 = taper[:, None, None] * taper[None, :, None] * taper[None, None, :]
    cosine, sine = fourier_tables(W)
    plane_cos, plane_sin = plane_tables(W)
    tables = (cosine, sine, plane_cos, plane_sin)
    factor = 4.0 / W**1.5 / W**3

    def transformed(fields, moves, depth_rel, col_rel):

        def windows(frame_field):

            def one_window(depth, column, move):
                return lax.dynamic_slice(
                    frame_field,
                    (H + depth * W + move[0], H + move[1], H + column * W + move[2]),
                    (W, W, W),
                )

            return jax.vmap(one_window)(depth_rel, col_rel, moves) * weight3

        cut = jax.vmap(windows)(fields)
        frame_total, count = (cut.shape[0], cut.shape[1])
        real_part, imag_part = forward(cut.reshape(frame_total * count, W, W, W), tables)
        return (
            real_part.reshape(frame_total, count, W, W * W),
            imag_part.reshape(frame_total, count, W, W * W),
        )

    columns = lax.all_to_all(
        column_pieces(volume), "brick", split_axis=2, concat_axis=1, tiled=True
    )
    following = from_behind(columns, "frame", -1)
    stacked = jnp.concatenate([columns, following], 0)
    stacked = merge_depth(stacked)
    local_count = offsets.shape[0]
    local_index = jnp.arange(local_count)
    depth_index = local_index % ZB
    column_local = local_index // ZB
    first = transformed(stacked[:frames_here], jnp.zeros_like(offsets), depth_index, column_local)
    second_re, second_im = transformed(stacked[1:], offsets, depth_index, column_local)
    paired_re = second_re[:-1] + second_re[1:]
    paired_im = second_im[:-1] + second_im[1:]
    spectrum_re, spectrum_im = cross_sum(first, (paired_re, paired_im))
    share_re, share_im = (
        lax.psum_scatter(spectrum_re, "frame", scatter_dimension=0, tiled=True),
        lax.psum_scatter(spectrum_im, "frame", scatter_dimension=0, tiled=True),
    )
    return inverse_real(share_re, share_im, tables) * factor


KB = 3
T = 8


def halves(table):
    table = np.asarray(table, np.float32)
    high = table.astype(ml_dtypes.bfloat16)
    low = (table - high.astype(np.float32)).astype(ml_dtypes.bfloat16)
    return np.stack([high, low])


def fixed_tables():
    index = np.arange(W)
    angle = 2.0 * np.pi * (index[:, None] * index[None, :] % W) / W
    cosine, sine = np.cos(angle), np.sin(angle)
    unit = np.eye(T)
    kept = np.zeros((KB * T, W))
    kept[: W // 2 + 1, : W // 2 + 1] = np.eye(W // 2 + 1)
    parts = np.stack([kept @ cosine, -(kept @ sine)]).reshape(2, KB, T, W)
    along_y = np.einsum("rbky,zs->rbzksy", parts, unit).reshape(2 * KB * T * T, T * W)
    weight = np.where((index == 0) | (index == W // 2), 1.0, 2.0)[:, None]
    factor = 4.0 / W**1.5 / W**3
    parts = factor * np.stack([kept @ (weight * cosine), -(kept @ (weight * sine))]).reshape(2, KB, T, W)
    back_y = np.einsum("rbky,zs->zyrbsk", parts, unit).reshape(T * W, 2 * KB * T * T)
    along_z = np.kron(np.block([[cosine, sine], [-sine, cosine]]), unit)
    four = np.eye(ZB)
    along_x = np.block([[np.kron(four, cosine), -np.kron(four, sine)], [np.kron(four, sine), np.kron(four, cosine)]])
    taper = 0.5 - 0.5 * np.cos(2.0 * np.pi * (index + 0.5) / W)
    lanes = np.tile(taper, ZB)
    weight3 = (taper[:, None, None] * taper[None, :, None] * lanes[None, None, :]).astype(np.float32)
    lane = np.arange(128)
    brick = np.arange(ZB)[:, None]
    main = (brick * 4 + lane // W) * 64 + lane % W + H
    edge = lane % 16
    halo = (brick * 4 + lane % 64 // 16) * 64 + np.where(edge < H, edge, edge + W)
    row_key = np.concatenate([main.reshape(-1), halo.reshape(-1)]).astype(np.int32)[:, None]
    return (
        halves(along_y), halves(along_z), halves(along_x),
        halves(along_x.T), halves(along_z.T), halves(back_y),
        weight3, row_key,
    )


def split(values):
    high = values.astype(jnp.bfloat16)
    return high, (values - high.astype(jnp.float32)).astype(jnp.bfloat16)


def mul(left, right):
    return jnp.dot(left, right, preferred_element_type=jnp.float32)


def from_left(table, values):
    high, low = split(values)
    return mul(table[0], high) + mul(table[0], low) + mul(table[1], high)


def from_right(values, table):
    high, low = split(values)
    return mul(high, table[0]) + mul(low, table[0]) + mul(high, table[1])


def pack_first(volume, send):
    for c in range(send.shape[0]):
        at = c * W
        parts = [volume[0, :, T * j : T * j + T, at : at + W] for j in range(4)]
        send[c] = jnp.concatenate(parts, -1)


def pack_second(volume, send):
    columns = send.shape[0]
    for c in range(columns):
        at = c * W
        parts = [volume[1, :, T * j : T * j + T, at : at + W] for j in range(4)]
        send[c, 0:T] = jnp.concatenate(parts, -1)
        parts = []
        for zh in range(2):
            for j in range(4):
                for start in (at - H, at + W):
                    if 0 <= start < columns * W:
                        parts.append(volume[1, 4 * zh : 4 * zh + 4, T * j : T * j + T, start : start + H])
                    else:
                        parts.append(jnp.zeros((4, T, H), jnp.float32))
        send[c, T:] = jnp.concatenate(parts, -1)


def first_windows(held, row_key, field):
    lane = lax.broadcasted_iota(jnp.int32, (1, 4 * 128), 1)
    col_key = (lane // W % 4 * 4 + lane // 128) * 64 + lane % W + H
    chosen = (row_key[0:512] == col_key).astype(jnp.float32).astype(jnp.bfloat16)
    rows = jnp.concatenate([held[4 * q : 4 * q + 4].reshape(W * T, 128) for q in range(ZB)], -1)
    high, low = split(rows)
    moved = mul(high, chosen) + mul(low, chosen)
    for j in range(4):
        field[:, T * j : T * j + T, :] = moved[:, 128 * j : 128 * j + 128].reshape(W, T, 128)


def second_windows(held, offsets, row_key, main, halo, spread, field):
    lane = lax.broadcasted_iota(jnp.int32, (1, 4 * 128), 1)
    brick = lane // W % 4
    shift = jnp.zeros((1, 4 * 128), jnp.int32)
    for q in range(ZB):
        shift = jnp.where(brick == q, offsets[q, 2], shift)
    col_key = (brick * 4 + lane // 128) * 64 + lane % W + H + shift
    chosen = (row_key[...] == col_key).astype(jnp.float32).astype(jnp.bfloat16)
    depth = main.shape[0] - 2 * H
    for ref in (main, halo):
        ref[0:H] = jnp.zeros((H, T, 128), jnp.float32)
        ref[H + depth :] = jnp.zeros((H, T, 128), jnp.float32)
    upper = lax.broadcasted_iota(jnp.int32, (1, 1, 1, 128), 3) >= 64
    main[H : H + depth] = held[:, 0:T].reshape(depth, T, 128)
    edges = held[:, T:]
    both = jnp.concatenate([jnp.where(upper, 0.0, edges), jnp.where(upper, edges, 0.0)], 1)
    halo[H : H + depth] = both.reshape(depth, T, 128)
    span = W + 2 * H
    rows = [ref[W * q : W * q + span].reshape(span * T, 128) for ref in (main, halo) for q in range(ZB)]
    high, low = split(jnp.concatenate(rows, -1))
    moved = mul(high, chosen) + mul(low, chosen)
    spread[:, 0:H] = jnp.zeros((span, H, 128), jnp.float32)
    spread[:, H + W :] = jnp.zeros((span, H, 128), jnp.float32)
    for j in range(4):
        spread[:, H + T * j : H + T * j + T] = moved[:, 128 * j : 128 * j + 128].reshape(span, T, 128)
    own = lax.broadcasted_iota(jnp.int32, (1, 1, 128), 2) // W
    cut = jnp.zeros((W, W, 128), jnp.float32)
    for q in range(ZB):
        window = spread[pl.ds(H + offsets[q, 0], W), pl.ds(H + offsets[q, 1], W), :]
        cut = jnp.where(own == q, window, cut)
    field[...] = cut


def to_depth(field, weight3, along_y, mid):
    block = T * T
    for zb in range(4):
        tapered = field[T * zb : T * zb + T] * weight3[T * zb : T * zb + T]
        part = from_left(along_y, tapered.reshape(T * W, 128))
        for r in range(2):
            for b in range(KB):
                at = (r * KB + b) * block
                mid[b, (r * 4 + zb) * block : (r * 4 + zb + 1) * block] = part[at : at + block]


def to_spectrum(lines, along_z, along_x):
    half = W * T
    spec = from_left(along_z, lines)
    return from_right(jnp.concatenate([spec[:half], spec[half:]], -1), along_x)


def exchange(volume, along_y, along_z, along_x, weight3, row_key, spectrum, held_second,
             send_first, send_second, held_first, field, mid, send_sem, recv_sem):
    count = send_first.shape[0]
    me = lax.axis_index("brick")
    steps = sorted(range(1, count), key=lambda k: (abs(k - count // 2), k))
    barrier = pltpu.get_barrier_semaphore()
    for k in steps:
        pl.semaphore_signal(
            barrier, inc=1, device_id={"brick": lax.rem(me + k, count)}, device_id_type=pl.DeviceIdType.MESH
        )
    pack_first(volume, send_first)
    pl.semaphore_wait(barrier, count - 1)

    def start(f, send, held):
        copies = []
        for k in steps:
            to = lax.rem(me + k, count)
            copy = pltpu.make_async_remote_copy(
                src_ref=send.at[to],
                dst_ref=held.at[me],
                send_sem=send_sem.at[f, k],
                recv_sem=recv_sem.at[f, k],
                device_id={"brick": to},
                device_id_type=pl.DeviceIdType.MESH,
            )
            copy.start()
            copies.append(copy)
        held[pl.ds(me, 1)] = send[pl.ds(me, 1)]
        return copies

    early = start(0, send_first, held_first)
    pack_second(volume, send_second)
    late = start(1, send_second, held_second)
    for copy in early:
        copy.wait()
    first_windows(held_first, row_key, field)
    to_depth(field, weight3, along_y, mid)
    for b in range(KB):
        spectrum[b] = to_spectrum(mid[b], along_z, along_x)
    for copy in late:
        copy.wait()


def correlate(offsets, first, held, along_y, along_z, along_x, back_x, back_z, back_y, weight3, row_key, out,
              main, halo, spread, field, mid, back):
    second_windows(held, offsets, row_key, main, halo, spread, field)
    to_depth(field, weight3, along_y, mid)
    block = T * T
    for b in range(KB):
        second = to_spectrum(mid[b], along_z, along_x)
        first_re, first_im = first[b, :, :128], first[b, :, 128:]
        second_re, second_im = second[:, :128], second[:, 128:]
        real_part = first_re * second_re + first_im * second_im
        imag_part = first_re * second_im - first_im * second_re
        lines = from_right(jnp.concatenate([real_part, imag_part], -1), back_x)
        part = from_left(back_z, jnp.concatenate([lines[:, :128], lines[:, 128:]], 0))
        for r in range(2):
            for zb in range(4):
                at = (r * 4 + zb) * block
                back[zb, (r * KB + b) * block : (r * KB + b + 1) * block] = part[at : at + block]
    for zb in range(4):
        result = from_left(back_y, back[zb]).reshape(T, W, 128)
        for q in range(ZB):
            out[q, T * zb : T * zb + T] = result[:, :, W * q : W * q + W]


def two_frames(volume, offsets):
    slabs = lax.axis_size("brick")
    planes = volume.shape[1]
    depth = slabs * planes
    rows = planes + planes // 2
    vmem = pl.BlockSpec(memory_space=pltpu.VMEM)
    along_y, along_z, along_x, back_x, back_z, back_y, weight3, row_key = map(jnp.asarray, fixed_tables())
    field = pltpu.VMEM((W, W, 128), jnp.float32)
    mid = pltpu.VMEM((KB, 2 * W * T, 128), jnp.float32)
    first, held = pl.pallas_call(
        exchange,
        out_shape=[
            jax.ShapeDtypeStruct((KB, W * T, 256), jnp.float32),
            jax.ShapeDtypeStruct((slabs, rows, T, 128), jnp.float32),
        ],
        in_specs=[vmem] * 6,
        out_specs=[vmem] * 2,
        scratch_shapes=[
            pltpu.VMEM((slabs, planes, T, 128), jnp.float32),
            pltpu.VMEM((slabs, rows, T, 128), jnp.float32),
            pltpu.VMEM((slabs, planes, T, 128), jnp.float32),
            field,
            mid,
            pltpu.SemaphoreType.DMA((2, slabs)),
            pltpu.SemaphoreType.DMA((2, slabs)),
        ],
        compiler_params=pltpu.CompilerParams(
            collective_id=0, has_side_effects=True, vmem_limit_bytes=32 << 20
        ),
    )(volume, along_y, along_z, along_x, weight3, row_key[:512])
    return pl.pallas_call(
        correlate,
        out_shape=jax.ShapeDtypeStruct((ZB, W, W, W), jnp.float32),
        in_specs=[pl.BlockSpec(memory_space=pltpu.SMEM)] + [vmem] * 10,
        out_specs=vmem,
        scratch_shapes=[
            pltpu.VMEM((depth + 2 * H, T, 128), jnp.float32),
            pltpu.VMEM((depth + 2 * H, T, 128), jnp.float32),
            pltpu.VMEM((W + 2 * H, W + 2 * H, 128), jnp.float32),
            field,
            mid,
            pltpu.VMEM((4, 2 * KB * T * T, 128), jnp.float32),
        ],
        compiler_params=pltpu.CompilerParams(vmem_limit_bytes=32 << 20),
    )(offsets, first, held, along_y, along_z, along_x, back_x, back_z, back_y, weight3, row_key)


def per_device(volume, offsets):
    slabs = lax.axis_size("brick")
    frames, planes, rows, cols = volume.shape
    short = lax.axis_size("frame") == 1 and frames == 2 and planes == T and rows == W
    if short and cols == slabs * W and slabs * planes == ZB * W and offsets.shape[0] == ZB:
        return two_frames(volume, offsets)
    return shards(volume, offsets)


def solution(mesh):
    return jax.shard_map(
        per_device,
        mesh=mesh,
        in_specs=(P(("groups", "frame"), "brick", None, None), P(("groups", "brick"), None)),
        out_specs=P(("groups", "brick", "frame"), None, None, None),
        check_vma=False,
    )
```

```python
import functools

import jax
import jax.numpy as jnp
import ml_dtypes
import numpy as np
from jax import lax
from jax.experimental import pallas as pl
from jax.experimental.pallas import tpu as pltpu
from jax.sharding import PartitionSpec as P

W = 32
H = 8
COLS_DEV = 1
ZB = 4


HIGHEST = lax.Precision.HIGHEST


def from_behind(shard, axis, by):
    count = lax.axis_size(axis)
    pairs = [(i, i + by) for i in range(count) if 0 <= i + by < count]
    return lax.ppermute(shard, axis, pairs)


def taper_table(width):
    position = jnp.arange(width).astype(jnp.float32)
    return 0.5 - 0.5 * jnp.cos(2.0 * jnp.pi * (position + 0.5) / width)


def fourier_tables(width):
    index = jnp.arange(width)
    product = index[:, None] * index[None, :] % width
    angle = 2.0 * jnp.pi * product.astype(jnp.float32) / width
    return (jnp.cos(angle), jnp.sin(angle))


def plane_tables(width):
    index = jnp.arange(width * width)
    upper = index // width
    lower = index % width
    product = (upper[:, None] * upper[None, :] + lower[:, None] * lower[None, :]) % width
    angle = 2.0 * jnp.pi * product.astype(jnp.float32) / width
    return (jnp.cos(angle), jnp.sin(angle))


def depth_apply(table, values):
    return jnp.einsum("kz,nzm->nkm", table, values, precision=HIGHEST)


def plane_apply(values, table):
    count, depth, plane = values.shape
    flat = values.reshape(count * depth, plane)
    result = jnp.dot(flat, table, precision=HIGHEST, preferred_element_type=jnp.float32)
    return result.reshape(count, depth, plane)


def forward(field, tables):
    cosine, sine, plane_cos, plane_sin = tables
    count, width = (field.shape[0], field.shape[1])
    values = field.reshape(count, width, width * width)
    real_part = plane_apply(values, plane_cos)
    imag_part = -plane_apply(values, plane_sin)
    return (
        depth_apply(cosine, real_part) + depth_apply(sine, imag_part),
        depth_apply(cosine, imag_part) - depth_apply(sine, real_part),
    )


def inverse_real(real_part, imag_part, tables):
    cosine, sine, plane_cos, plane_sin = tables
    first_re = depth_apply(cosine, real_part) - depth_apply(sine, imag_part)
    first_im = depth_apply(cosine, imag_part) + depth_apply(sine, real_part)
    result = plane_apply(first_re, plane_cos) - plane_apply(first_im, plane_sin)
    width = result.shape[1]
    return result.reshape(result.shape[0], width, width, width)


def column_pieces(slabs):
    count, planes, rows, cols = slabs.shape
    span = COLS_DEV * W
    tiles = slabs.reshape(count, planes, rows // W, W, cols // span, span)
    tiles = jnp.pad(tiles, ((0, 0), (0, 0), (1, 1), (0, 0), (1, 1), (0, 0)))
    tall = jnp.concatenate([tiles[:, :, :-2, W - H :], tiles[:, :, 1:-1], tiles[:, :, 2:, :H]], 3)
    wide = jnp.concatenate(
        [tall[:, :, :, :, :-2, span - H :], tall[:, :, :, :, 1:-1], tall[:, :, :, :, 2:, :H]], 5
    )
    wide = jnp.transpose(wide, (0, 1, 2, 4, 3, 5))
    owners = rows // W * (cols // span)
    return wide.reshape(count, planes, owners, (W + 2 * H) * (span + 2 * H))


def merge_depth(received):
    count = received.shape[0]
    depth_total = received.shape[1] * received.shape[2]
    merged = received.reshape(count, depth_total, W + 2 * H, COLS_DEV * W + 2 * H)
    return jnp.pad(merged, ((0, 0), (H, H), (0, 0), (0, 0)))


def cross_sum(first, paired):
    first_re, first_im = first
    paired_re, paired_im = paired
    spectrum_re = jnp.sum(first_re * paired_re + first_im * paired_im, axis=0)
    spectrum_im = jnp.sum(first_re * paired_im - first_im * paired_re, axis=0)
    return (spectrum_re, spectrum_im)


def shards(volume, offsets):
    frames_here = volume.shape[0]
    taper = taper_table(W)
    weight3 = taper[:, None, None] * taper[None, :, None] * taper[None, None, :]
    cosine, sine = fourier_tables(W)
    plane_cos, plane_sin = plane_tables(W)
    tables = (cosine, sine, plane_cos, plane_sin)
    factor = 4.0 / W**1.5 / W**3

    def transformed(fields, moves, depth_rel, col_rel):

        def windows(frame_field):

            def one_window(depth, column, move):
                return lax.dynamic_slice(
                    frame_field,
                    (H + depth * W + move[0], H + move[1], H + column * W + move[2]),
                    (W, W, W),
                )

            return jax.vmap(one_window)(depth_rel, col_rel, moves) * weight3

        cut = jax.vmap(windows)(fields)
        frame_total, count = (cut.shape[0], cut.shape[1])
        real_part, imag_part = forward(cut.reshape(frame_total * count, W, W, W), tables)
        return (
            real_part.reshape(frame_total, count, W, W * W),
            imag_part.reshape(frame_total, count, W, W * W),
        )

    columns = lax.all_to_all(
        column_pieces(volume), "brick", split_axis=2, concat_axis=1, tiled=True
    )
    following = from_behind(columns, "frame", -1)
    stacked = jnp.concatenate([columns, following], 0)
    stacked = merge_depth(stacked)
    local_count = offsets.shape[0]
    local_index = jnp.arange(local_count)
    depth_index = local_index % ZB
    column_local = local_index // ZB
    first = transformed(stacked[:frames_here], jnp.zeros_like(offsets), depth_index, column_local)
    second_re, second_im = transformed(stacked[1:], offsets, depth_index, column_local)
    paired_re = second_re[:-1] + second_re[1:]
    paired_im = second_im[:-1] + second_im[1:]
    spectrum_re, spectrum_im = cross_sum(first, (paired_re, paired_im))
    share_re, share_im = (
        lax.psum_scatter(spectrum_re, "frame", scatter_dimension=0, tiled=True),
        lax.psum_scatter(spectrum_im, "frame", scatter_dimension=0, tiled=True),
    )
    return inverse_real(share_re, share_im, tables) * factor


KB = 3
T = 8


def halves(table):
    table = np.asarray(table, np.float32)
    high = table.astype(ml_dtypes.bfloat16)
    low = (table - high.astype(np.float32)).astype(ml_dtypes.bfloat16)
    return np.stack([high, low])


def fixed_tables():
    index = np.arange(W)
    angle = 2.0 * np.pi * (index[:, None] * index[None, :] % W) / W
    cosine, sine = np.cos(angle), np.sin(angle)
    unit = np.eye(T)
    kept = np.zeros((KB * T, W))
    kept[: W // 2 + 1, : W // 2 + 1] = np.eye(W // 2 + 1)
    parts = np.stack([kept @ cosine, -(kept @ sine)]).reshape(2, KB, T, W)
    along_y = np.einsum("rbky,zs->rbzksy", parts, unit).reshape(2 * KB * T * T, T * W)
    weight = np.where((index == 0) | (index == W // 2), 1.0, 2.0)[:, None]
    factor = 4.0 / W**1.5 / W**3
    parts = factor * np.stack([kept @ (weight * cosine), -(kept @ (weight * sine))]).reshape(2, KB, T, W)
    back_y = np.einsum("rbky,zs->zyrbsk", parts, unit).reshape(T * W, 2 * KB * T * T)
    along_z = np.kron(np.concatenate([cosine, sine]), unit)
    four = np.eye(ZB)
    along_x = np.block([[np.kron(four, cosine), -np.kron(four, sine)], [np.kron(four, sine), np.kron(four, cosine)]])
    taper = 0.5 - 0.5 * np.cos(2.0 * np.pi * (index + 0.5) / W)
    lanes = np.tile(taper, ZB)
    weight3 = (taper[:, None, None] * taper[None, :, None] * lanes[None, None, :]).astype(np.float32)
    moved = np.einsum("qp,jk,xw->qjxkpw", four, four, np.eye(W)).reshape(512, 512).astype(ml_dtypes.bfloat16)
    return (
        halves(along_y), halves(along_z), halves(along_x),
        halves(along_x.T), halves(back_y), weight3, moved,
    )


def split(values):
    high = values.astype(jnp.bfloat16)
    return high, (values - high.astype(jnp.float32)).astype(jnp.bfloat16)


def mul(left, right):
    return jnp.dot(left, right, preferred_element_type=jnp.float32)


def from_left(table, values):
    high, low = split(values)
    return mul(table[0], high) + mul(table[0], low) + mul(table[1], high)


def from_right(values, table):
    high, low = split(values)
    return mul(high, table[0]) + mul(low, table[0]) + mul(high, table[1])


def pack_first(volume, send):
    for c in range(send.shape[0]):
        at = c * W
        parts = [volume[0, :, T * j : T * j + T, at : at + W] for j in range(4)]
        send[c] = jnp.concatenate(parts, -1)


def pack_second(volume, send):
    columns = send.shape[0]
    for c in range(columns):
        at = c * W
        parts = [volume[1, :, T * j : T * j + T, at : at + W] for j in range(4)]
        send[c, 0:T] = jnp.concatenate(parts, -1)
        parts = []
        for zh in range(2):
            for j in range(4):
                for start in (at - H, at + W):
                    if 0 <= start < columns * W:
                        parts.append(volume[1, 4 * zh : 4 * zh + 4, T * j : T * j + T, start : start + H])
                    else:
                        parts.append(jnp.zeros((4, T, H), jnp.float32))
        send[c, T:] = jnp.concatenate(parts, -1)


def first_windows(held, chosen, field):
    rows = jnp.concatenate([held[4 * q : 4 * q + 4].reshape(W * T, 128) for q in range(ZB)], -1)
    high, low = split(rows)
    moved = mul(high, chosen) + mul(low, chosen)
    for j in range(4):
        field[:, T * j : T * j + T, :] = moved[:, 128 * j : 128 * j + 128].reshape(W, T, 128)


def second_windows(held, offsets, main, halo, spread, field):
    lane = lax.broadcasted_iota(jnp.int32, (1, 128), 1)
    brick = lane >> 5
    shift = jnp.zeros((1, 128), jnp.int32)
    for q in range(ZB):
        shift = jnp.where(brick == q, offsets[q, 2], shift)
    col_key = brick * 256 + (lane & 31) + H + shift
    row = lax.broadcasted_iota(jnp.int32, (512, 128), 0)
    owner = (row >> 7) * 256
    edge = row & 15
    main_key = owner + ((row >> 5) & 3) * 64 + (row & 31) + H
    halo_key = owner + ((row >> 4) & 3) * 64 + jnp.where(edge < H, edge, edge + W)
    chosen = jnp.concatenate([
        jnp.concatenate([(key == col_key + 64 * j).astype(jnp.float32).astype(jnp.bfloat16) for j in range(4)], -1)
        for key in (main_key, halo_key)
    ], 0)
    depth = main.shape[0] - 2 * H
    for ref in (main, halo):
        ref[0:H] = jnp.zeros((H, T, 128), jnp.float32)
        ref[H + depth :] = jnp.zeros((H, T, 128), jnp.float32)
    upper = lax.broadcasted_iota(jnp.int32, (1, 1, 1, 128), 3) >= 64
    main[H : H + depth] = held[:, 0:T].reshape(depth, T, 128)
    edges = held[:, T:]
    both = jnp.concatenate([jnp.where(upper, 0.0, edges), jnp.where(upper, edges, 0.0)], 1)
    halo[H : H + depth] = both.reshape(depth, T, 128)
    span = W + 2 * H
    rows = [ref[W * q : W * q + span].reshape(span * T, 128) for ref in (main, halo) for q in range(ZB)]
    high, low = split(jnp.concatenate(rows, -1))
    moved = mul(high, chosen) + mul(low, chosen)
    spread[:, 0:H] = jnp.zeros((span, H, 128), jnp.float32)
    spread[:, H + W :] = jnp.zeros((span, H, 128), jnp.float32)
    for j in range(4):
        spread[:, H + T * j : H + T * j + T] = moved[:, 128 * j : 128 * j + 128].reshape(span, T, 128)
    own = lax.broadcasted_iota(jnp.int32, (1, 1, 128), 2) // W
    cut = jnp.zeros((W, W, 128), jnp.float32)
    for q in range(ZB):
        window = spread[pl.ds(H + offsets[q, 0], W), pl.ds(H + offsets[q, 1], W), :]
        cut = jnp.where(own == q, window, cut)
    field[...] = cut


def to_depth(field, weight3, along_y, mid):
    block = T * T
    for pair in range(2):
        depths = (2 * pair, 2 * pair + 1)
        tapered = [(field[T * zb : T * zb + T] * weight3[T * zb : T * zb + T]).reshape(T * W, 128) for zb in depths]
        part = from_left(along_y, jnp.concatenate(tapered, -1))
        for s, zb in enumerate(depths):
            for r in range(2):
                for b in range(KB):
                    at = (r * KB + b) * block
                    mid[b, zb * block : (zb + 1) * block, 128 * r : 128 * r + 128] = part[
                        at : at + block, 128 * s : 128 * s + 128
                    ]


def cos_sin(along_z, lines):
    both = from_left(along_z, lines)
    cosine, sine = both[: W * T], both[W * T :]
    return cosine[:, :128], cosine[:, 128:], sine[:, :128], sine[:, 128:]


def to_spectrum(lines, along_z, along_x):
    cos_re, cos_im, sin_re, sin_im = cos_sin(along_z, lines)
    return from_right(jnp.concatenate([cos_re + sin_im, cos_im - sin_re], -1), along_x)


def fetch(sources, targets, sems):
    copies = [pltpu.make_async_copy(s, t, sems.at[i]) for i, (s, t) in enumerate(zip(sources, targets))]
    for copy in copies:
        copy.start()
    return copies


def exchange(voxels, *refs):
    outside, (spectrum, held_second), refs = refs[:5], refs[5:7], refs[7:]
    tables, (volume, send_first, send_second, held_first, field, mid, own_sem, table_sem, send_sem, recv_sem) = refs[:5], refs[5:]
    along_y, along_z, along_x, weight3, chosen = tables
    frames = fetch([voxels.at[f] for f in range(2)], [volume.at[f] for f in range(2)], own_sem)
    count = send_first.shape[0]
    me = lax.axis_index("brick")
    steps = sorted(range(1, count), key=lambda k: (abs(k - count // 2), k))
    barrier = pltpu.get_barrier_semaphore()
    for k in steps:
        pl.semaphore_signal(
            barrier, inc=1, device_id={"brick": lax.rem(me + k, count)}, device_id_type=pl.DeviceIdType.MESH
        )
    frames[0].wait()
    pack_first(volume, send_first)
    pl.semaphore_wait(barrier, count - 1)

    def start(f, send, held):
        copies = []
        for k in steps:
            to = lax.rem(me + k, count)
            copy = pltpu.make_async_remote_copy(
                src_ref=send.at[to],
                dst_ref=held.at[me],
                send_sem=send_sem.at[f, k],
                recv_sem=recv_sem.at[f, k],
                device_id={"brick": to},
                device_id_type=pl.DeviceIdType.MESH,
            )
            copy.start()
            copies.append(copy)
        held[pl.ds(me, 1)] = send[pl.ds(me, 1)]
        return copies

    early = start(0, send_first, held_first)
    frames[1].wait()
    pack_second(volume, send_second)
    late = start(1, send_second, held_second)
    for copy in fetch(outside, tables, table_sem):
        copy.wait()
    for copy in early:
        copy.wait()
    first_windows(held_first, chosen[...], field)
    to_depth(field, weight3, along_y, mid)
    for b in range(KB):
        spectrum[b] = to_spectrum(mid[b], along_z, along_x)
    for copy in late:
        copy.wait()


def correlate(first, held, *refs):
    outside, out, refs = refs[:7], refs[7], refs[8:]
    inside, (main, halo, spread, field, mid, back, sems) = refs[:7], refs[7:]
    copies = fetch(outside, inside, sems)
    offsets, along_y, along_z, along_x, back_x, back_y, weight3 = inside
    copies[0].wait()
    second_windows(held, offsets, main, halo, spread, field)
    for copy in copies[1:]:
        copy.wait()
    to_depth(field, weight3, along_y, mid)
    block = T * T
    for b in range(KB):
        second = to_spectrum(mid[b], along_z, along_x)
        first_re, first_im = first[b, :, :128], first[b, :, 128:]
        second_re, second_im = second[:, :128], second[:, 128:]
        real_part = first_re * second_re + first_im * second_im
        imag_part = first_re * second_im - first_im * second_re
        lines = from_right(jnp.concatenate([real_part, imag_part], -1), back_x)
        cos_re, cos_im, sin_re, sin_im = cos_sin(along_z, lines)
        for r, part in enumerate((cos_re - sin_im, cos_im + sin_re)):
            at = (r * KB + b) * block
            for zb in range(4):
                half = 128 * (zb % 2)
                back[zb // 2, at : at + block, half : half + 128] = part[zb * block : (zb + 1) * block]
    for pair in range(2):
        results = from_left(back_y, back[pair])
        for s in range(2):
            zb = 2 * pair + s
            result = results[:, 128 * s : 128 * s + 128].reshape(T, W, 128)
            for q in range(ZB):
                out[q, T * zb : T * zb + T] = result[:, :, W * q : W * q + W]


def two_frames(volume, offsets):
    slabs = lax.axis_size("brick")
    planes = volume.shape[1]
    depth = slabs * planes
    rows = planes + planes // 2
    vmem = pl.BlockSpec(memory_space=pltpu.VMEM)
    hbm = pl.BlockSpec(memory_space=pltpu.HBM)
    tables = [jnp.asarray(table) for table in fixed_tables()]
    along_y, along_z, along_x, back_x, back_y, weight3, moved = tables
    early = (along_y, along_z, along_x, weight3, moved)
    late = (along_y, along_z, along_x, back_x, back_y, weight3)
    field = pltpu.VMEM((W, W, 128), jnp.float32)
    mid = pltpu.VMEM((KB, W * T, 256), jnp.float32)
    first, held = pl.pallas_call(
        exchange,
        out_shape=[
            jax.ShapeDtypeStruct((KB, W * T, 256), jnp.float32),
            jax.ShapeDtypeStruct((slabs, rows, T, 128), jnp.float32),
        ],
        in_specs=[hbm] * (1 + len(early)),
        out_specs=[vmem] * 2,
        scratch_shapes=[
            *[pltpu.VMEM(table.shape, table.dtype) for table in early],
            pltpu.VMEM(volume.shape, jnp.float32),
            pltpu.VMEM((slabs, planes, T, 128), jnp.float32),
            pltpu.VMEM((slabs, rows, T, 128), jnp.float32),
            pltpu.VMEM((slabs, planes, T, 128), jnp.float32),
            field,
            mid,
            pltpu.SemaphoreType.DMA((2,)),
            pltpu.SemaphoreType.DMA((len(early),)),
            pltpu.SemaphoreType.DMA((2, slabs)),
            pltpu.SemaphoreType.DMA((2, slabs)),
        ],
        compiler_params=pltpu.CompilerParams(
            collective_id=0, has_side_effects=True, vmem_limit_bytes=63 << 20
        ),
    )(volume, *early)
    return pl.pallas_call(
        correlate,
        out_shape=jax.ShapeDtypeStruct((ZB, W, W, W), jnp.float32),
        in_specs=[vmem] * 2 + [hbm] * (1 + len(late)),
        out_specs=vmem,
        scratch_shapes=[
            pltpu.SMEM(offsets.shape, jnp.int32),
            *[pltpu.VMEM(table.shape, table.dtype) for table in late],
            pltpu.VMEM((depth + 2 * H, T, 128), jnp.float32),
            pltpu.VMEM((depth + 2 * H, T, 128), jnp.float32),
            pltpu.VMEM((W + 2 * H, W + 2 * H, 128), jnp.float32),
            field,
            mid,
            pltpu.VMEM((2, 2 * KB * T * T, 256), jnp.float32),
            pltpu.SemaphoreType.DMA((1 + len(late),)),
        ],
        compiler_params=pltpu.CompilerParams(vmem_limit_bytes=63 << 20),
    )(first, held, offsets, *late)


def per_device(volume, offsets):
    slabs = lax.axis_size("brick")
    frames, planes, rows, cols = volume.shape
    short = lax.axis_size("frame") == 1 and frames == 2 and planes == T and rows == W
    if short and cols == slabs * W and slabs * planes == ZB * W and offsets.shape[0] == ZB:
        return two_frames(volume, offsets)
    return shards(volume, offsets)


def solution(mesh):
    return jax.shard_map(
        per_device,
        mesh=mesh,
        in_specs=(P(("groups", "frame"), "brick", None, None), P(("groups", "brick"), None)),
        out_specs=P(("groups", "brick", "frame"), None, None, None),
        check_vma=False,
    )
```

```python
import functools

import jax
import jax.numpy as jnp
import ml_dtypes
import numpy as np
from jax import lax
from jax.experimental import pallas as pl
from jax.experimental.pallas import tpu as pltpu
from jax.sharding import PartitionSpec as P

W = 32
H = 8
COLS_DEV = 1
ZB = 4


HIGHEST = lax.Precision.HIGHEST


def from_behind(shard, axis, by):
    count = lax.axis_size(axis)
    pairs = [(i, i + by) for i in range(count) if 0 <= i + by < count]
    return lax.ppermute(shard, axis, pairs)


def taper_table(width):
    position = jnp.arange(width).astype(jnp.float32)
    return 0.5 - 0.5 * jnp.cos(2.0 * jnp.pi * (position + 0.5) / width)


def fourier_tables(width):
    index = jnp.arange(width)
    product = index[:, None] * index[None, :] % width
    angle = 2.0 * jnp.pi * product.astype(jnp.float32) / width
    return (jnp.cos(angle), jnp.sin(angle))


def plane_tables(width):
    index = jnp.arange(width * width)
    upper = index // width
    lower = index % width
    product = (upper[:, None] * upper[None, :] + lower[:, None] * lower[None, :]) % width
    angle = 2.0 * jnp.pi * product.astype(jnp.float32) / width
    return (jnp.cos(angle), jnp.sin(angle))


def depth_apply(table, values):
    return jnp.einsum("kz,nzm->nkm", table, values, precision=HIGHEST)


def plane_apply(values, table):
    count, depth, plane = values.shape
    flat = values.reshape(count * depth, plane)
    result = jnp.dot(flat, table, precision=HIGHEST, preferred_element_type=jnp.float32)
    return result.reshape(count, depth, plane)


def forward(field, tables):
    cosine, sine, plane_cos, plane_sin = tables
    count, width = (field.shape[0], field.shape[1])
    values = field.reshape(count, width, width * width)
    real_part = plane_apply(values, plane_cos)
    imag_part = -plane_apply(values, plane_sin)
    return (
        depth_apply(cosine, real_part) + depth_apply(sine, imag_part),
        depth_apply(cosine, imag_part) - depth_apply(sine, real_part),
    )


def inverse_real(real_part, imag_part, tables):
    cosine, sine, plane_cos, plane_sin = tables
    first_re = depth_apply(cosine, real_part) - depth_apply(sine, imag_part)
    first_im = depth_apply(cosine, imag_part) + depth_apply(sine, real_part)
    result = plane_apply(first_re, plane_cos) - plane_apply(first_im, plane_sin)
    width = result.shape[1]
    return result.reshape(result.shape[0], width, width, width)


def column_pieces(slabs):
    count, planes, rows, cols = slabs.shape
    span = COLS_DEV * W
    tiles = slabs.reshape(count, planes, rows // W, W, cols // span, span)
    tiles = jnp.pad(tiles, ((0, 0), (0, 0), (1, 1), (0, 0), (1, 1), (0, 0)))
    tall = jnp.concatenate([tiles[:, :, :-2, W - H :], tiles[:, :, 1:-1], tiles[:, :, 2:, :H]], 3)
    wide = jnp.concatenate(
        [tall[:, :, :, :, :-2, span - H :], tall[:, :, :, :, 1:-1], tall[:, :, :, :, 2:, :H]], 5
    )
    wide = jnp.transpose(wide, (0, 1, 2, 4, 3, 5))
    owners = rows // W * (cols // span)
    return wide.reshape(count, planes, owners, (W + 2 * H) * (span + 2 * H))


def merge_depth(received):
    count = received.shape[0]
    depth_total = received.shape[1] * received.shape[2]
    merged = received.reshape(count, depth_total, W + 2 * H, COLS_DEV * W + 2 * H)
    return jnp.pad(merged, ((0, 0), (H, H), (0, 0), (0, 0)))


def cross_sum(first, paired):
    first_re, first_im = first
    paired_re, paired_im = paired
    spectrum_re = jnp.sum(first_re * paired_re + first_im * paired_im, axis=0)
    spectrum_im = jnp.sum(first_re * paired_im - first_im * paired_re, axis=0)
    return (spectrum_re, spectrum_im)


def shards(volume, offsets):
    frames_here = volume.shape[0]
    taper = taper_table(W)
    weight3 = taper[:, None, None] * taper[None, :, None] * taper[None, None, :]
    cosine, sine = fourier_tables(W)
    plane_cos, plane_sin = plane_tables(W)
    tables = (cosine, sine, plane_cos, plane_sin)
    factor = 4.0 / W**1.5 / W**3

    def transformed(fields, moves, depth_rel, col_rel):

        def windows(frame_field):

            def one_window(depth, column, move):
                return lax.dynamic_slice(
                    frame_field,
                    (H + depth * W + move[0], H + move[1], H + column * W + move[2]),
                    (W, W, W),
                )

            return jax.vmap(one_window)(depth_rel, col_rel, moves) * weight3

        cut = jax.vmap(windows)(fields)
        frame_total, count = (cut.shape[0], cut.shape[1])
        real_part, imag_part = forward(cut.reshape(frame_total * count, W, W, W), tables)
        return (
            real_part.reshape(frame_total, count, W, W * W),
            imag_part.reshape(frame_total, count, W, W * W),
        )

    columns = lax.all_to_all(
        column_pieces(volume), "brick", split_axis=2, concat_axis=1, tiled=True
    )
    following = from_behind(columns, "frame", -1)
    stacked = jnp.concatenate([columns, following], 0)
    stacked = merge_depth(stacked)
    local_count = offsets.shape[0]
    local_index = jnp.arange(local_count)
    depth_index = local_index % ZB
    column_local = local_index // ZB
    first = transformed(stacked[:frames_here], jnp.zeros_like(offsets), depth_index, column_local)
    second_re, second_im = transformed(stacked[1:], offsets, depth_index, column_local)
    paired_re = second_re[:-1] + second_re[1:]
    paired_im = second_im[:-1] + second_im[1:]
    spectrum_re, spectrum_im = cross_sum(first, (paired_re, paired_im))
    share_re, share_im = (
        lax.psum_scatter(spectrum_re, "frame", scatter_dimension=0, tiled=True),
        lax.psum_scatter(spectrum_im, "frame", scatter_dimension=0, tiled=True),
    )
    return inverse_real(share_re, share_im, tables) * factor


KB = 3
T = 8


def halves(table):
    table = np.asarray(table, np.float32)
    high = table.astype(ml_dtypes.bfloat16)
    low = (table - high.astype(np.float32)).astype(ml_dtypes.bfloat16)
    return np.stack([high, low])


def fixed_tables():
    index = np.arange(W)
    angle = 2.0 * np.pi * (index[:, None] * index[None, :] % W) / W
    cosine, sine = np.cos(angle), np.sin(angle)
    unit = np.eye(T)
    kept = np.zeros((KB * T, W))
    kept[: W // 2 + 1, : W // 2 + 1] = np.eye(W // 2 + 1)
    parts = np.stack([kept @ cosine, -(kept @ sine)]).reshape(2, KB, T, W)
    along_y = np.einsum("rbky,zs->rbzksy", parts, unit).reshape(2 * KB * T * T, T * W)
    weight = np.where((index == 0) | (index == W // 2), 1.0, 2.0)[:, None]
    factor = 4.0 / W**1.5 / W**3
    parts = factor * np.stack([kept @ (weight * cosine), -(kept @ (weight * sine))]).reshape(2, KB, T, W)
    back_y = np.einsum("rbky,zs->zyrbsk", parts, unit).reshape(T * W, 2 * KB * T * T)
    along_z = np.kron(np.concatenate([cosine, sine]), unit)
    four = np.eye(ZB)
    along_x = np.block([[np.kron(four, cosine), -np.kron(four, sine)], [np.kron(four, sine), np.kron(four, cosine)]])
    taper = 0.5 - 0.5 * np.cos(2.0 * np.pi * (index + 0.5) / W)
    lanes = np.tile(taper, ZB)
    weight3 = (taper[:, None, None] * taper[None, :, None] * lanes[None, None, :]).astype(np.float32)
    moved = np.einsum("qp,jk,xw->qjxkpw", four, four, np.eye(W)).reshape(512, 512).astype(ml_dtypes.bfloat16)
    return (
        halves(along_y), halves(along_z), halves(along_x),
        halves(along_x.T), halves(back_y), weight3, moved,
    )


def split(values):
    high = values.astype(jnp.bfloat16)
    return high, (values - high.astype(jnp.float32)).astype(jnp.bfloat16)


def mul(left, right):
    return jnp.dot(left, right, preferred_element_type=jnp.float32)


def from_left(table, values):
    high, low = split(values)
    return mul(table[0], high) + mul(table[0], low) + mul(table[1], high)


def from_right(values, table):
    high, low = split(values)
    return mul(high, table[0]) + mul(low, table[0]) + mul(high, table[1])


def pack_first(volume, send):
    for c in range(send.shape[0]):
        at = c * W
        parts = [volume[0, :, T * j : T * j + T, at : at + W] for j in range(4)]
        send[c] = jnp.concatenate(parts, -1)


def pack_second(volume, send):
    columns = send.shape[0]
    for c in range(columns):
        at = c * W
        parts = [volume[1, :, T * j : T * j + T, at : at + W] for j in range(4)]
        send[c, 0:T] = jnp.concatenate(parts, -1)
        parts = []
        for zh in range(2):
            for j in range(4):
                for start in (at - H, at + W):
                    if 0 <= start < columns * W:
                        parts.append(volume[1, 4 * zh : 4 * zh + 4, T * j : T * j + T, start : start + H])
                    else:
                        parts.append(jnp.zeros((4, T, H), jnp.float32))
        send[c, T:] = jnp.concatenate(parts, -1)


def first_windows(held, chosen, field):
    rows = jnp.concatenate([held[4 * q : 4 * q + 4].reshape(W * T, 128) for q in range(ZB)], -1)
    high, low = split(rows)
    moved = mul(high, chosen) + mul(low, chosen)
    for j in range(4):
        field[:, T * j : T * j + T, :] = moved[:, 128 * j : 128 * j + 128].reshape(W, T, 128)


def second_windows(held, offsets, main, halo, spread, field):
    lane = lax.broadcasted_iota(jnp.int32, (1, 128), 1)
    brick = lane >> 5
    shift = jnp.zeros((1, 128), jnp.int32)
    for q in range(ZB):
        shift = jnp.where(brick == q, offsets[q, 2], shift)
    col_key = brick * 256 + (lane & 31) + H + shift
    row = lax.broadcasted_iota(jnp.int32, (512, 128), 0)
    owner = (row >> 7) * 256
    edge = row & 15
    main_key = owner + ((row >> 5) & 3) * 64 + (row & 31) + H
    halo_key = owner + ((row >> 4) & 3) * 64 + jnp.where(edge < H, edge, edge + W)
    chosen = jnp.concatenate([
        jnp.concatenate([(key == col_key + 64 * j).astype(jnp.float32).astype(jnp.bfloat16) for j in range(4)], -1)
        for key in (main_key, halo_key)
    ], 0)
    depth = main.shape[0] - 2 * H
    for ref in (main, halo):
        ref[0:H] = jnp.zeros((H, T, 128), jnp.float32)
        ref[H + depth :] = jnp.zeros((H, T, 128), jnp.float32)
    upper = lax.broadcasted_iota(jnp.int32, (1, 1, 1, 128), 3) >= 64
    main[H : H + depth] = held[:, 0:T].reshape(depth, T, 128)
    edges = held[:, T:]
    both = jnp.concatenate([jnp.where(upper, 0.0, edges), jnp.where(upper, edges, 0.0)], 1)
    halo[H : H + depth] = both.reshape(depth, T, 128)
    span = W + 2 * H
    rows = [ref[W * q : W * q + span].reshape(span * T, 128) for ref in (main, halo) for q in range(ZB)]
    high, low = split(jnp.concatenate(rows, -1))
    moved = mul(high, chosen) + mul(low, chosen)
    spread[:, 0:H] = jnp.zeros((span, H, 128), jnp.float32)
    spread[:, H + W :] = jnp.zeros((span, H, 128), jnp.float32)
    for j in range(4):
        spread[:, H + T * j : H + T * j + T] = moved[:, 128 * j : 128 * j + 128].reshape(span, T, 128)
    own = lax.broadcasted_iota(jnp.int32, (1, 1, 128), 2) // W
    cut = jnp.zeros((W, W, 128), jnp.float32)
    for q in range(ZB):
        window = spread[pl.ds(H + offsets[q, 0], W), pl.ds(H + offsets[q, 1], W), :]
        cut = jnp.where(own == q, window, cut)
    field[...] = cut


def to_depth(field, weight3, along_y, mid):
    block = T * T
    for pair in range(2):
        depths = (2 * pair, 2 * pair + 1)
        tapered = [(field[T * zb : T * zb + T] * weight3[T * zb : T * zb + T]).reshape(T * W, 128) for zb in depths]
        part = from_left(along_y, jnp.concatenate(tapered, -1))
        for s, zb in enumerate(depths):
            for r in range(2):
                for b in range(KB):
                    at = (r * KB + b) * block
                    mid[b, zb * block : (zb + 1) * block, 128 * r : 128 * r + 128] = part[
                        at : at + block, 128 * s : 128 * s + 128
                    ]


def cos_sin(along_z, lines):
    both = from_left(along_z, lines)
    cosine, sine = both[: W * T], both[W * T :]
    return cosine[:, :128], cosine[:, 128:], sine[:, :128], sine[:, 128:]


def to_spectrum(lines, along_z, along_x):
    cos_re, cos_im, sin_re, sin_im = cos_sin(along_z, lines)
    return from_right(jnp.concatenate([cos_re + sin_im, cos_im - sin_re], -1), along_x)


def fetch(sources, targets, sems):
    copies = [pltpu.make_async_copy(s, t, sems.at[i]) for i, (s, t) in enumerate(zip(sources, targets))]
    for copy in copies:
        copy.start()
    return copies


def exchange(voxels, *refs):
    outside, (spectrum_out, held_second), refs = refs[:5], refs[5:7], refs[7:]
    tables, (volume, send_first, send_second, held_first, field, mid, spectrum, own_sem, table_sem, send_sem, recv_sem) = refs[:5], refs[5:]
    along_y, along_z, along_x, weight3, chosen = tables
    frames = fetch([voxels.at[f] for f in range(2)], [volume.at[f] for f in range(2)], own_sem)
    count = send_first.shape[0]
    me = lax.axis_index("brick")
    steps = sorted(range(1, count), key=lambda k: (abs(k - count // 2), k))
    barrier = pltpu.get_barrier_semaphore()
    for k in steps:
        pl.semaphore_signal(
            barrier, inc=1, device_id={"brick": lax.rem(me + k, count)}, device_id_type=pl.DeviceIdType.MESH
        )
    frames[0].wait()
    pack_first(volume, send_first)
    pl.semaphore_wait(barrier, count - 1)

    def start(f, send, held):
        copies = []
        for k in steps:
            to = lax.rem(me + k, count)
            copy = pltpu.make_async_remote_copy(
                src_ref=send.at[to],
                dst_ref=held.at[me],
                send_sem=send_sem.at[f, k],
                recv_sem=recv_sem.at[f, k],
                device_id={"brick": to},
                device_id_type=pl.DeviceIdType.MESH,
            )
            copy.start()
            copies.append(copy)
        own = pltpu.make_async_copy(send.at[me], held.at[me], send_sem.at[f, 0])
        own.start()
        return copies + [own]

    early = start(0, send_first, held_first)
    frames[1].wait()
    pack_second(volume, send_second)
    late = start(1, send_second, held_second)
    for copy in fetch(outside, tables, table_sem):
        copy.wait()
    for copy in early:
        copy.wait()
    first_windows(held_first, chosen[...], field)
    to_depth(field, weight3, along_y, mid)
    for b in range(KB):
        spectrum[b] = to_spectrum(mid[b], along_z, along_x)
    late.append(pltpu.make_async_copy(spectrum, spectrum_out, recv_sem.at[0, 0]))
    late[-1].start()
    for copy in late:
        copy.wait()


def correlate(held, *refs):
    outside, out, refs = refs[:8], refs[8], refs[9:]
    inside, (main, halo, spread, field, mid, back, done, sems, out_sems) = refs[:8], refs[8:]
    copies = fetch(outside, inside, sems)
    offsets, along_y, along_z, along_x, back_x, back_y, weight3, first = inside
    copies[0].wait()
    second_windows(held, offsets, main, halo, spread, field)
    for copy in copies[1:]:
        copy.wait()
    to_depth(field, weight3, along_y, mid)
    block = T * T
    for b in range(KB):
        second = to_spectrum(mid[b], along_z, along_x)
        first_re, first_im = first[b, :, :128], first[b, :, 128:]
        second_re, second_im = second[:, :128], second[:, 128:]
        real_part = first_re * second_re + first_im * second_im
        imag_part = first_re * second_im - first_im * second_re
        lines = from_right(jnp.concatenate([real_part, imag_part], -1), back_x)
        cos_re, cos_im, sin_re, sin_im = cos_sin(along_z, lines)
        for r, part in enumerate((cos_re - sin_im, cos_im + sin_re)):
            at = (r * KB + b) * block
            for zb in range(4):
                half = 128 * (zb % 2)
                back[zb // 2, at : at + block, half : half + 128] = part[zb * block : (zb + 1) * block]
    leaving = []
    for pair in range(2):
        results = from_left(back_y, back[pair])
        for s in range(2):
            zb = 2 * pair + s
            result = results[:, 128 * s : 128 * s + 128].reshape(T, W, 128)
            for q in range(ZB):
                done[q, T * zb : T * zb + T] = result[:, :, W * q : W * q + W]
        half = pl.ds(2 * T * pair, 2 * T)
        leaving.append(pltpu.make_async_copy(done.at[:, half], out.at[:, half], out_sems.at[pair]))
        leaving[-1].start()
    for copy in leaving:
        copy.wait()


def two_frames(volume, offsets):
    slabs = lax.axis_size("brick")
    planes = volume.shape[1]
    depth = slabs * planes
    rows = planes + planes // 2
    vmem = pl.BlockSpec(memory_space=pltpu.VMEM)
    hbm = pl.BlockSpec(memory_space=pltpu.HBM)
    tables = [jnp.asarray(table) for table in fixed_tables()]
    along_y, along_z, along_x, back_x, back_y, weight3, moved = tables
    early = (along_y, along_z, along_x, weight3, moved)
    late = (along_y, along_z, along_x, back_x, back_y, weight3)
    field = pltpu.VMEM((W, W, 128), jnp.float32)
    mid = pltpu.VMEM((KB, W * T, 256), jnp.float32)
    first, held = pl.pallas_call(
        exchange,
        out_shape=[
            jax.ShapeDtypeStruct((KB, W * T, 256), jnp.float32),
            jax.ShapeDtypeStruct((slabs, rows, T, 128), jnp.float32),
        ],
        in_specs=[hbm] * (1 + len(early)),
        out_specs=[hbm] * 2,
        scratch_shapes=[
            *[pltpu.VMEM(table.shape, table.dtype) for table in early],
            pltpu.VMEM(volume.shape, jnp.float32),
            pltpu.VMEM((slabs, planes, T, 128), jnp.float32),
            pltpu.VMEM((slabs, rows, T, 128), jnp.float32),
            pltpu.VMEM((slabs, planes, T, 128), jnp.float32),
            field,
            mid,
            pltpu.VMEM((KB, W * T, 256), jnp.float32),
            pltpu.SemaphoreType.DMA((2,)),
            pltpu.SemaphoreType.DMA((len(early),)),
            pltpu.SemaphoreType.DMA((2, slabs)),
            pltpu.SemaphoreType.DMA((2, slabs)),
        ],
        compiler_params=pltpu.CompilerParams(
            collective_id=0, has_side_effects=True, vmem_limit_bytes=63 << 20
        ),
    )(volume, *early)
    late += (first,)
    return pl.pallas_call(
        correlate,
        out_shape=jax.ShapeDtypeStruct((ZB, W, W, W), jnp.float32),
        in_specs=[vmem] + [hbm] * (1 + len(late)),
        out_specs=hbm,
        scratch_shapes=[
            pltpu.SMEM(offsets.shape, jnp.int32),
            *[pltpu.VMEM(table.shape, table.dtype) for table in late],
            pltpu.VMEM((depth + 2 * H, T, 128), jnp.float32),
            pltpu.VMEM((depth + 2 * H, T, 128), jnp.float32),
            pltpu.VMEM((W + 2 * H, W + 2 * H, 128), jnp.float32),
            field,
            mid,
            pltpu.VMEM((2, 2 * KB * T * T, 256), jnp.float32),
            pltpu.VMEM((ZB, W, W, W), jnp.float32),
            pltpu.SemaphoreType.DMA((1 + len(late),)),
            pltpu.SemaphoreType.DMA((2,)),
        ],
        compiler_params=pltpu.CompilerParams(vmem_limit_bytes=63 << 20),
    )(held, offsets, *late)


def per_device(volume, offsets):
    slabs = lax.axis_size("brick")
    frames, planes, rows, cols = volume.shape
    short = lax.axis_size("frame") == 1 and frames == 2 and planes == T and rows == W
    if short and cols == slabs * W and slabs * planes == ZB * W and offsets.shape[0] == ZB:
        return two_frames(volume, offsets)
    return shards(volume, offsets)


def solution(mesh):
    return jax.shard_map(
        per_device,
        mesh=mesh,
        in_specs=(P(("groups", "frame"), "brick", None, None), P(("groups", "brick"), None)),
        out_specs=P(("groups", "brick", "frame"), None, None, None),
        check_vma=False,
    )
```
